32 devices in a mesh: gx: 4 (over y, core), gy: 2 (over x), gz: 4 (over z).
Axes of the slice: x: 2, y: 2, z: 4, core: 2. Of those that a mesh axis runs over, the one named last changes fastest.
Arguments:
- positions: float32 [4, 2, 4, 3, 1024], P('gx', 'gy', 'gz'), may hold values from 0 to 1
- types: int32 [4, 2, 4, 1024], P('gx', 'gy', 'gz'), may hold values from 0 to 3
- tile_lists: int32 [8, 36], replicated, may hold values from 0 to 215, as said below
- hardness: float32 [4], replicated, may hold values from 2 to 8
- electroneg: float32 [4], replicated, may hold values from 2 to 8
- gamma_table: float32 [4], replicated, may hold values from 0.25 to 1
Outputs:
- charges: float32 [4, 2, 4, 1024], P('gx', 'gy', 'gz')
- solutions: float32 [4, 2, 4, 2, 1024], P('gx', 'gy', 'gz')
The draws below stay inside these ranges and needn't reach their ends.
Inputs may be any that keep to these rules, and one draw needn't show every extreme that they name: `tile_lists`: entry (t, o, u) stands in tile t's list as often as entry (u, 26 - o, t) stands in tile u's list; every offset o of 0 to 26 occurs; the lists are the same for every box.
All inputs are finite; a program needn't handle non-finite values.
Results may differ from the reference program's by a relative error of at most 0.0003.
Values sent between devices are 32-bit elements; how exact they have to be, the bound alone decides.
A program may use at most 64 MiB of HBM per device.

```python
import math
import jax
import jax.numpy as jnp
from jax import lax

TILES = 8
NBR = 36
NTYPES = 4
ITERS = 4
ATOMS = 1024
BX = 4
BY = 2
BZ = 4


def draw_tile_lists(key, part):
    half = NBR // 2
    first_key = jax.random.fold_in(key, 11)
    second_key = jax.random.fold_in(key, 23)
    orders = jax.vmap(lambda single: jax.random.permutation(single, TILES))(jax.random.split(first_key, half))
    orders = orders.astype(jnp.int32)
    offsets = (jax.random.permutation(second_key, half * TILES).astype(jnp.int32) % 27).reshape(half, TILES)
    forward = offsets * TILES + orders
    inverse = jnp.argsort(orders, axis=1, stable=True).astype(jnp.int32)
    back_offsets = 26 - jnp.take_along_axis(offsets, inverse, axis=1)
    backward = back_offsets * TILES + inverse
    return jnp.concatenate([forward, backward], axis=0).T.astype(jnp.int32)


def with_ends(values, rng, least, high):
    index_at = [jax.random.randint(jax.random.fold_in(rng, axis), (), 0, length) for axis, length in enumerate(values.shape)]
    widest = values.shape.index(max(values.shape))
    next_to = index_at[:widest] + [(index_at[widest] + 1) % values.shape[widest]] + index_at[widest + 1:]
    return values.at[tuple(index_at)].set(least).at[tuple(next_to)].set(high)


def block_scale(key, shape, pieces, low, top_value):
    level = 1.0
    for position, blocks in pieces:
        heights = jax.random.uniform(jax.random.fold_in(jax.random.fold_in(key, 6), position), (blocks,), jnp.float32, low / len(pieces), top_value / len(pieces))
        level = level * jnp.repeat(jnp.exp(heights), shape[position] // blocks).reshape((-1,) + (1,) * (len(shape) - 1 - position))
    return level


def setup_inputs(seed: int = 0) -> dict:
    key_list = jax.random.split(jax.random.key(seed), 7)
    positions = jnp.clip(1.0 * jax.random.uniform(key_list[0], (BX, BY, BZ, 3, ATOMS), jnp.float32) ** block_scale(key_list[0], (BX, BY, BZ, 3, ATOMS), ((0, 4), (1, 2), (2, 4)), -0.2, 0.2), 0.0, 1.0)
    types = with_ends(jax.random.randint(key_list[1], (BX, BY, BZ, ATOMS), 0, NTYPES), jax.random.fold_in(key_list[1], 1), 0, NTYPES - 1).astype(jnp.int32)
    tile_lists = draw_tile_lists(jax.random.fold_in(key_list[6], 71), 0)
    hardness = jnp.clip(jnp.exp(jax.random.uniform(key_list[3], (NTYPES,), jnp.float32, math.log(2.0), math.log(8.0))), 2.0, 8.0)
    electroneg = jnp.clip(jax.random.uniform(key_list[4], (NTYPES,), jnp.float32, 2.0, 8.0), 2.0, 8.0)
    gamma_table = jnp.clip(jnp.exp(jax.random.uniform(key_list[5], (NTYPES,), jnp.float32, math.log(0.25), math.log(1.0))), 0.25, 1.0)
    return {"positions": positions, "types": types, "tile_lists": tile_lists, "hardness": hardness, "electroneg": electroneg, "gamma_table": gamma_table}


CUTOFF = 10.0
COULOMB = 0.3
VOLUME = 10.0

def taper(scaled):
    return scaled ** 4 * (((20.0 * scaled - 70.0) * scaled + 84.0) * scaled - 35.0) + 1.0

def atom_table(types, table):
    kinds = jnp.arange(table.shape[0], dtype=jnp.int32)
    onehot = (types[..., None] == kinds).astype(jnp.float32)
    return jnp.dot(onehot, table, precision=lax.Precision.HIGHEST)

def tile_blocks(nearby, tile_lists, box_edge):
    tile_count = tile_lists.shape[0]
    tile_width = nearby.shape[2]
    local_data = nearby[:, 13 * tile_count:14 * tile_count]
    diagonal_mask = jnp.arange(tile_width)[:, None] == jnp.arange(tile_width)[None, :]

    def one_tile(inputs):
        mine_data, entries, tile_index = inputs
        others = nearby[:, entries]
        offset_box = entries // tile_count
        shifts = jnp.stack([offset_box // 9 - 1, offset_box // 3 % 3 - 1, offset_box % 3 - 1]).astype(jnp.float32)
        separation = (others[:3, :, None, :] + shifts[:, :, None, None] - mine_data[:3, None, :, None]) * box_edge
        spacing = jnp.sqrt(lax.optimization_barrier(jnp.sum(separation * separation, axis=0)))
        present = others[4][:, None, :]
        gamma_other = others[3] + (1.0 - others[4])
        inverse_cube = (mine_data[3][None, :, None] * gamma_other[:, None, :]) ** (-1.5)
        shielding = jnp.cbrt(spacing * spacing * spacing + inverse_cube)
        tapered = jnp.where(spacing < CUTOFF, taper(spacing / CUTOFF), 0.0)
        coupling = COULOMB * tapered / shielding * present
        itself = (entries == 13 * tile_count + tile_index)[:, None, None] & diagonal_mask[None]
        return jnp.where(itself, 0.0, coupling)
    mine_all = jnp.transpose(local_data, (1, 0, 2))
    return lax.map(one_tile, (mine_all, tile_lists, jnp.arange(tile_count, dtype=jnp.int32)))

def couple(blocks, nearby_vectors, tile_lists):
    picked = nearby_vectors[:, tile_lists]
    return jnp.einsum('teij,ktej->kti', blocks, picked, precision=lax.Precision.HIGHEST)

def reference(positions, types, tile_lists, hardness, electroneg, gamma_table):
    grid = positions.shape[:3]
    atoms = positions.shape[4]
    tile_count = tile_lists.shape[0]
    tile_width = atoms // tile_count
    box_edge = (atoms * VOLUME) ** (1.0 / 3.0)
    hardness_atom = atom_table(types, hardness)
    electro_atom = atom_table(types, electroneg)
    gamma_atom = atom_table(types, gamma_table)
    present = jnp.ones_like(gamma_atom)
    atom_data = jnp.concatenate([positions, gamma_atom[:, :, :, None], present[:, :, :, None]], axis=3)
    box_total = grid[0] * grid[1] * grid[2]
    box_ids = jnp.arange(box_total, dtype=jnp.int32)

    def padding(field):
        return jnp.pad(field, ((1, 1), (1, 1), (1, 1), (0, 0), (0, 0)))

    def gather_box(padded, box):
        first = (box // (grid[1] * grid[2])).astype(jnp.int32)
        second = (box // grid[2] % grid[1]).astype(jnp.int32)
        third = (box % grid[2]).astype(jnp.int32)
        anchor = jnp.zeros((), jnp.int32)
        piece = lax.dynamic_slice(padded, (first, second, third, anchor, anchor), (3, 3, 3) + padded.shape[3:])
        channels = padded.shape[3]
        arranged = jnp.transpose(piece.reshape(27, channels, tile_count, tile_width), (1, 0, 2, 3))
        return arranged.reshape(channels, 27 * tile_count, tile_width)
    padded_data = padding(atom_data)

    def box_blocks(box):
        return tile_blocks(gather_box(padded_data, box), tile_lists, box_edge)
    blocks = lax.map(box_blocks, box_ids)

    def apply(vectors):
        padded = padding(vectors)
        systems = vectors.shape[3]

        def one_box(inputs):
            box_matrix, box = inputs
            return couple(box_matrix, gather_box(padded, box), tile_lists).reshape(systems, atoms)
        coupled = lax.map(one_box, (blocks, box_ids)).reshape(vectors.shape)
        return hardness_atom[:, :, :, None, :] * vectors + coupled

    def total(field):
        return lax.optimization_barrier(jnp.sum(field, axis=(0, 1, 2, 4)))[:, None]
    right = jnp.stack([-electro_atom, -jnp.ones_like(electro_atom)], axis=3)
    solution = jnp.zeros_like(right)
    residual = right
    direction = right
    norm_now = total(residual * residual)
    for iteration in range(ITERS):
        image = apply(direction)
        alpha = norm_now / total(direction * image)
        solution = solution + alpha * direction
        residual = residual - alpha * image
        norm_next = total(residual * residual)
        direction = residual + norm_next / norm_now * direction
        norm_now = norm_next
    sums = lax.optimization_barrier(jnp.sum(solution, axis=(0, 1, 2, 4)))
    charges = solution[:, :, :, 0] - sums[0] / sums[1] * solution[:, :, :, 1]
    return (charges, solution)
```

```python
import functools
import math

import jax
import jax.numpy as jnp
from jax import lax
from jax.experimental import pallas as pl
from jax.experimental.pallas import tpu as pltpu
from jax.sharding import PartitionSpec as P

ITERS = 4
CUTOFF = 10.0
COULOMB = 0.3
VOLUME = 10.0
MESH = pl.DeviceIdType.MESH
AXES = ("gx", "gy", "gz")
FAR = 100.0
DEPTH = 48


def total(a):
    return jnp.sum(jnp.sum(a, axis=0, keepdims=True), axis=1, keepdims=True)


def split(a):
    first = a.astype(jnp.bfloat16)
    rest = a - first.astype(jnp.float32)
    second = rest.astype(jnp.bfloat16)
    third = (rest - second.astype(jnp.float32)).astype(jnp.bfloat16)
    return [p.astype(jnp.float32) for p in (first, second, third)]


def kernel(
    grid, unroll, lists, hardness, electroneg, gamma, geo,
    charges, solution_ref,
    geo_halo, vec_halos, shares, features, lhs, weights, weight_col,
    current0, current1, eta_rows, gamma_rows, diagonal, image0, image1, blocks,
    geo_send, geo_recv, vec_sends, vec_recvs, sum_sends, sum_recvs,
):
    tiles, nbr = lists.shape
    kinds = gamma.shape[0]
    width = geo.shape[2]
    devices = math.prod(grid)
    scale = (tiles * width * VOLUME) ** (1.0 / 3.0) / CUTOFF
    me = [lax.axis_index(a) for a in AXES]
    my_id = (me[0] * grid[1] + me[1]) * grid[2] + me[2]

    def device_of(d):
        return (d // (grid[1] * grid[2]), (d // grid[2]) % grid[1], d % grid[2])

    def neighbour(o):
        where = (me[0] + o // 9 - 1, me[1] + (o // 3) % 3 - 1, me[2] + o % 3 - 1)
        there = functools.reduce(
            jnp.logical_and,
            [jnp.logical_and(w >= 0, w < g) for w, g in zip(where, grid)],
        )
        return where, there

    barrier = pltpu.get_barrier_semaphore()

    @pl.loop(1, devices)
    def _(j):
        d = lax.rem(my_id + j, devices)
        pl.semaphore_signal(barrier, inc=1, device_id=device_of(d), device_id_type=MESH)

    pl.semaphore_wait(barrier, devices - 1)

    def halo_copy(buffer, send, recv, slot, o, where):
        return pltpu.make_async_remote_copy(
            src_ref=buffer.at[13],
            dst_ref=buffer.at[slot],
            send_sem=send.at[o],
            recv_sem=recv.at[slot],
            device_id=where,
            device_id_type=MESH,
        )

    def each_neighbour(do):
        @pl.loop(0, 27)
        def _(o):
            where, there = neighbour(o)

            @pl.when(jnp.logical_and(there, o != 13))
            def _():
                do(o, where)

    def start_halo(buffer, send, recv):
        each_neighbour(lambda o, w: halo_copy(buffer, send, recv, 26 - o, o, w).start())

    def end_send(buffer, send, recv):
        each_neighbour(lambda o, w: halo_copy(buffer, send, recv, 26 - o, o, w).wait_send())

    def sum_copy(k, slot, j):
        return pltpu.make_async_remote_copy(
            src_ref=shares[k].at[0],
            dst_ref=shares[k].at[slot],
            send_sem=sum_sends[k].at[j],
            recv_sem=sum_recvs[k].at[slot],
            device_id=device_of(lax.rem(my_id + j, devices)),
            device_id_type=MESH,
        )

    def each_other(do):
        @pl.loop(1, devices)
        def _(j):
            do(j)

    geo_halo[13] = geo[...]
    start_halo(geo_halo, geo_send, geo_recv)

    row = lax.broadcasted_iota(jnp.int32, (8, width), 0)
    lane = lax.broadcasted_iota(jnp.int32, (1, width), 1)

    def look_up(table, kind):
        value = jnp.full(kind.shape, table[0], jnp.float32)
        for k in range(1, kinds):
            value = jnp.where(kind == float(k), table[k], value)
        return value

    def prepare(o, mine):
        where, there = neighbour(o)
        shift = [(o // 9 - 1), (o // 3) % 3 - 1, o % 3 - 1]
        shift = [s.astype(jnp.float32) - 0.5 if not mine else jnp.float32(-0.5) for s in shift]
        shifts = jnp.where(row == 0, shift[0], jnp.where(row == 1, shift[1], shift[2]))
        for pair in range(tiles // 2):
            data = jnp.where(there, geo_halo[o, pair], 0.0)
            gammas = look_up(gamma, data)
            w8 = jnp.exp2(jnp.log(gammas) * (-1.5 / math.log(2.0))) * CUTOFF**-1.5
            chi8 = jnp.where(there, -look_up(electroneg, data), 0.0)
            if mine:
                eta8 = look_up(hardness, data)
            for half in range(2):
                u = pair * 2 + half
                entry = o * tiles + u
                r3 = half * 4 + 3
                raw = data if half == 0 else pltpu.roll(data, 4, 0)
                at = (raw + shifts) * scale
                norm = jnp.sum(jnp.where(row < 3, at * at, 0.0), axis=0, keepdims=True)
                norm = jnp.where(there, norm, FAR)
                at = jnp.where(there, at, 0.0)
                b = jnp.where(row < 3, -2.0 * at, jnp.where(row == 3, 1.0, jnp.where(row == 4, norm, 0.0)))
                b1, b2, b3 = split(b)
                features[entry] = jnp.concatenate([b1, b2, b1, b2, b3, b1], axis=0).astype(jnp.bfloat16)
                weights[pl.ds(entry, 1), :] = w8[r3 : r3 + 1]
                current0[pl.ds(entry, 1), :] = chi8[r3 : r3 + 1]
                current1[pl.ds(entry, 1), :] = jnp.where(there, jnp.full((1, width), -1.0, jnp.float32), 0.0)
                if mine:
                    a = jnp.where(row < 3, at, jnp.where(row == 3, norm, jnp.where(row == 4, 1.0, 0.0)))
                    a1, a2, a3 = split(a)
                    rows = jnp.concatenate(
                        [a1, a1, a2, a2, a1, a3, jnp.zeros((width - DEPTH, width), jnp.float32)], axis=0
                    )
                    lhs[u] = jnp.transpose(rows).astype(jnp.bfloat16)
                    weight_col[u] = jnp.transpose(jnp.broadcast_to(w8[r3 : r3 + 1], (width, width)))
                    eta_rows[pl.ds(u, 1), :] = eta8[r3 : r3 + 1]
                    gamma_rows[pl.ds(u, 1), :] = gammas[r3 : r3 + 1]

    prepare(13, True)

    @pl.loop(0, 27)
    def _(o):
        where, there = neighbour(o)

        @pl.when(jnp.logical_and(there, o != 13))
        def _():
            halo_copy(geo_halo, geo_send, geo_recv, o, o, where).wait_recv()

        @pl.when(o != 13)
        def _():
            prepare(o, False)

    lanes_zero = jnp.zeros((width, width), jnp.float32)

    def row_sum(acc):
        return jnp.sum(jnp.transpose(acc), axis=0, keepdims=True)

    @pl.loop(0, tiles)
    def _(t):
        mine = lhs[t][:, :DEPTH]

        def step(g, carry):
            acc0, acc1, selves = carry
            for i in range(unroll):
                e = g * unroll + i
                entry = lists[t, e]
                x2 = jnp.dot(mine, features[entry], preferred_element_type=jnp.float32)
                x2 = jnp.maximum(x2, 1e-10)
                x = x2 * lax.rsqrt(x2)
                c = x2 * x + weight_col[t] * weights[pl.ds(entry, 1), :]
                inverse = jnp.exp2(jnp.log(c) * (-1.0 / (3.0 * math.log(2.0))))
                near = jnp.maximum(1.0 - x, 0.0)
                near = near * near
                f = COULOMB / CUTOFF
                taper = ((20.0 * f * x + 10.0 * f) * x + 4.0 * f) * x + f
                h = (near * near) * (taper * inverse)
                blocks[t * nbr + e] = h
                acc0 = acc0 + h * current0[pl.ds(entry, 1), :]
                acc1 = acc1 - h
                selves = selves + jnp.where(entry == 13 * tiles + t, 1, 0)
            return acc0, acc1, selves

        acc0, acc1, selves = lax.fori_loop(
            0, nbr // unroll, step, (lanes_zero, lanes_zero, jnp.int32(0))
        )
        image0[pl.ds(t, 1), :] = row_sum(acc0)
        image1[pl.ds(t, 1), :] = row_sum(acc1)
        diagonal[pl.ds(t, 1), :] = (
            eta_rows[pl.ds(t, 1), :]
            - selves.astype(jnp.float32) * COULOMB * gamma_rows[pl.ds(t, 1), :]
        )

    def couple():
        @pl.loop(0, tiles)
        def _(t):
            def step(g, carry):
                acc0, acc1 = carry
                for i in range(unroll):
                    e = g * unroll + i
                    entry = lists[t, e]
                    h = blocks[t * nbr + e]
                    acc0 = acc0 + h * current0[pl.ds(entry, 1), :]
                    acc1 = acc1 + h * current1[pl.ds(entry, 1), :]
                return acc0, acc1

            acc0, acc1 = lax.fori_loop(0, nbr // unroll, step, (lanes_zero, lanes_zero))
            image0[pl.ds(t, 1), :] = row_sum(acc0)
            image1[pl.ds(t, 1), :] = row_sum(acc1)

    systems = range(2)
    images = (image0, image1)
    currents = (current0, current1)
    diag = diagonal[...]
    r = [c[pl.ds(13 * tiles, tiles), :] for c in currents]
    w = [diag * r[s] + images[s][...] for s in systems]
    p = along = deep = None
    x = [jnp.zeros_like(r[0]) for s in systems]
    sum_x = [jnp.zeros((1, 1), jnp.float32) for s in systems]
    sum_p = rr_old = alpha = None
    for k in range(ITERS):
        parts = [
            jnp.where(
                lane == 0, total(r[s] * r[s]),
                jnp.where(lane == 1, total(r[s] * w[s]), jnp.where(lane == 2, total(r[s]), 0.0)),
            )
            for s in systems
        ]
        shares[k][0] = jnp.concatenate(parts, axis=0)
        last = k + 1 == ITERS
        if not last:
            buffer, send, recv = vec_halos[k], vec_sends[k], vec_recvs[k]
            for s in systems:
                buffer[13, s] = w[s]
            start_halo(buffer, send, recv)
        each_other(lambda j: sum_copy(k, devices - j, j).start())
        if not last:
            @pl.loop(0, 27)
            def _(o):
                where, there = neighbour(o)

                @pl.when(jnp.logical_and(there, o != 13))
                def _():
                    halo_copy(buffer, send, recv, o, o, where).wait_recv()

                start = pl.multiple_of(o * tiles, tiles)
                for s in systems:
                    currents[s][pl.ds(start, tiles), :] = jnp.where(there, buffer[o, s], 0.0)

            couple()
            q = [diag * w[s] + images[s][...] for s in systems]
        each_other(lambda j: sum_copy(k, j, j).wait_recv())
        sums = jnp.sum(shares[k][...], axis=0)
        rr, rw, sr = [
            [jnp.sum(jnp.where(lane == i, sums[s : s + 1], 0.0), axis=1, keepdims=True) for s in systems]
            for i in range(3)
        ]
        if k == 0:
            alpha = [rr[s] / rw[s] for s in systems]
            p, along, sum_p = list(r), list(w), sr
            if not last:
                deep = q
        else:
            beta = [rr[s] / rr_old[s] for s in systems]
            alpha = [rr[s] / (rw[s] - beta[s] * rr[s] / alpha[s]) for s in systems]
            p = [r[s] + beta[s] * p[s] for s in systems]
            sum_p = [sr[s] + beta[s] * sum_p[s] for s in systems]
            if not last:
                along = [w[s] + beta[s] * along[s] for s in systems]
                deep = [q[s] + beta[s] * deep[s] for s in systems]
        x = [x[s] + alpha[s] * p[s] for s in systems]
        sum_x = [sum_x[s] + alpha[s] * sum_p[s] for s in systems]
        rr_old = rr
        if not last:
            r = [r[s] - alpha[s] * along[s] for s in systems]
            w = [w[s] - alpha[s] * deep[s] for s in systems]

    for s in systems:
        solution_ref[s] = x[s]
    charges[...] = x[0] - (sum_x[0] / sum_x[1]) * x[1]

    end_send(geo_halo, geo_send, geo_recv)
    for k in range(ITERS - 1):
        end_send(vec_halos[k], vec_sends[k], vec_recvs[k])
    for k in range(ITERS):
        each_other(lambda j: sum_copy(k, devices - j, j).wait_send())


def on_device(positions, types, tile_lists, hardness, electroneg, gamma_table):
    atoms = positions.shape[4]
    tiles, nbr = tile_lists.shape
    width = atoms // tiles
    grid = tuple(lax.axis_size(a) for a in AXES)
    devices = math.prod(grid)
    unroll = next(u for u in (4, 3, 2, 1) if nbr % u == 0)
    geo = jnp.concatenate(
        [
            jnp.transpose(positions.reshape(3, tiles, width), (1, 0, 2)),
            types.reshape(tiles, 1, width).astype(jnp.float32),
        ],
        axis=1,
    ).reshape(tiles // 2, 8, width)
    f32 = jnp.float32
    vmem = pl.BlockSpec(memory_space=pltpu.VMEM)
    smem = pl.BlockSpec(memory_space=pltpu.SMEM)
    rounds = ITERS - 1
    charges, solution_ = pl.pallas_call(
        functools.partial(kernel, grid, unroll),
        out_shape=(
            jax.ShapeDtypeStruct((tiles, width), f32),
            jax.ShapeDtypeStruct((2, tiles, width), f32),
        ),
        in_specs=[smem] * 4 + [vmem],
        out_specs=(vmem, vmem),
        scratch_shapes=[
            pltpu.VMEM((27, tiles // 2, 8, width), f32),
            [pltpu.VMEM((27, 2, tiles, width), f32)] * rounds,
            [pltpu.VMEM((devices, 2, width), f32)] * ITERS,
            pltpu.VMEM((27 * tiles, DEPTH, width), jnp.bfloat16),
            pltpu.VMEM((tiles, width, width), jnp.bfloat16),
            pltpu.VMEM((27 * tiles, width), f32),
            pltpu.VMEM((tiles, width, width), f32),
            pltpu.VMEM((27 * tiles, width), f32),
            pltpu.VMEM((27 * tiles, width), f32),
            pltpu.VMEM((tiles, width), f32),
            pltpu.VMEM((tiles, width), f32),
            pltpu.VMEM((tiles, width), f32),
            pltpu.VMEM((tiles, width), f32),
            pltpu.VMEM((tiles, width), f32),
            pltpu.VMEM((tiles * nbr, width, width), f32),
            pltpu.SemaphoreType.DMA((27,)),
            pltpu.SemaphoreType.DMA((27,)),
            [pltpu.SemaphoreType.DMA((27,))] * rounds,
            [pltpu.SemaphoreType.DMA((27,))] * rounds,
            [pltpu.SemaphoreType.DMA((devices,))] * ITERS,
            [pltpu.SemaphoreType.DMA((devices,))] * ITERS,
        ],
        compiler_params=pltpu.CompilerParams(
            collective_id=0, has_side_effects=True, vmem_limit_bytes=56 * 2**20
        ),
    )(tile_lists, hardness, electroneg, gamma_table, geo)
    return charges.reshape(1, 1, 1, atoms), solution_.reshape(1, 1, 1, 2, atoms)


def solution(mesh):
    in_specs = (P("gx", "gy", "gz", None, None), P("gx", "gy", "gz", None), P(), P(), P(), P())
    out_specs = (P("gx", "gy", "gz", None), P("gx", "gy", "gz", None, None))
    return jax.shard_map(
        on_device, mesh=mesh, in_specs=in_specs, out_specs=out_specs, check_vma=False
    )
```

```python
import functools
import math

import jax
import jax.numpy as jnp
from jax import lax
from jax.experimental import pallas as pl
from jax.experimental.pallas import tpu as pltpu
from jax.sharding import PartitionSpec as P

ITERS = 4
CUTOFF = 10.0
COULOMB = 0.3
VOLUME = 10.0
MESH = pl.DeviceIdType.MESH
AXES = ("gx", "gy", "gz")
FAR = 100.0
DEPTH = 48


def total(a):
    return jnp.sum(jnp.sum(a, axis=0, keepdims=True), axis=1, keepdims=True)


def split(a):
    first = a.astype(jnp.bfloat16)
    rest = a - first.astype(jnp.float32)
    second = rest.astype(jnp.bfloat16)
    third = (rest - second.astype(jnp.float32)).astype(jnp.bfloat16)
    return [p.astype(jnp.float32) for p in (first, second, third)]


def kernel(
    grid, unroll, lists, hardness, electroneg, gamma, positions, types,
    charges, solution_ref,
    geo_halo, vec_halos, shares, features, lhs, weights, weight_col,
    current0, current1, eta_rows, gamma_rows, diagonal, image0, image1, blocks,
    geo_send, geo_recv, vec_sends, vec_recvs, sum_sends, sum_recvs,
):
    tiles, nbr = lists.shape
    kinds = gamma.shape[0]
    width = types.shape[3] // tiles
    devices = math.prod(grid)
    scale = (tiles * width * VOLUME) ** (1.0 / 3.0) / CUTOFF
    me = [lax.axis_index(a) for a in AXES]
    my_id = (me[0] * grid[1] + me[1]) * grid[2] + me[2]

    def device_of(d):
        return (d // (grid[1] * grid[2]), (d // grid[2]) % grid[1], d % grid[2])

    def neighbour(o):
        where = (me[0] + o // 9 - 1, me[1] + (o // 3) % 3 - 1, me[2] + o % 3 - 1)
        there = functools.reduce(
            jnp.logical_and,
            [jnp.logical_and(w >= 0, w < g) for w, g in zip(where, grid)],
        )
        return where, there

    barrier = pltpu.get_barrier_semaphore()

    @pl.loop(1, devices)
    def _(j):
        d = lax.rem(my_id + j, devices)
        pl.semaphore_signal(barrier, inc=1, device_id=device_of(d), device_id_type=MESH)


    def halo_copy(buffer, send, recv, slot, o, where):
        return pltpu.make_async_remote_copy(
            src_ref=buffer.at[13],
            dst_ref=buffer.at[slot],
            send_sem=send.at[o],
            recv_sem=recv.at[slot],
            device_id=where,
            device_id_type=MESH,
        )

    def each_neighbour(do):
        @pl.loop(0, 27)
        def _(o):
            where, there = neighbour(o)

            @pl.when(jnp.logical_and(there, o != 13))
            def _():
                do(o, where)

    def start_halo(buffer, send, recv):
        each_neighbour(lambda o, w: halo_copy(buffer, send, recv, 26 - o, o, w).start())

    def end_send(buffer, send, recv):
        each_neighbour(lambda o, w: halo_copy(buffer, send, recv, 26 - o, o, w).wait_send())

    def sum_copy(k, slot, j):
        return pltpu.make_async_remote_copy(
            src_ref=shares[k].at[0],
            dst_ref=shares[k].at[slot],
            send_sem=sum_sends[k],
            recv_sem=sum_recvs[k],
            device_id=device_of(lax.rem(my_id + j, devices)),
            device_id_type=MESH,
        )

    def wait_shares(k, sem):
        rest = shares[k].at[pl.ds(1, devices - 1)]
        pltpu.make_async_copy(rest, rest, sem).wait()

    def each_other(do):
        @pl.loop(1, devices)
        def _(j):
            do(j)

    for u in range(tiles):
        pair, top, span = u // 2, u % 2 * 4, slice(u * width, (u + 1) * width)
        geo_halo[13, pair, top : top + 3, :] = positions[0, 0, 0, :, span]
        geo_halo[13, pair, top + 3 : top + 4, :] = types[0, 0, :, span].astype(jnp.float32)

    row = lax.broadcasted_iota(jnp.int32, (8, width), 0)
    lane = lax.broadcasted_iota(jnp.int32, (1, width), 1)

    def look_up(table, kind):
        value = jnp.full(kind.shape, table[0], jnp.float32)
        for k in range(1, kinds):
            value = jnp.where(kind == float(k), table[k], value)
        return value

    def prepare(o, mine):
        where, there = neighbour(o)
        shift = [(o // 9 - 1), (o // 3) % 3 - 1, o % 3 - 1]
        shift = [s.astype(jnp.float32) - 0.5 if not mine else jnp.float32(-0.5) for s in shift]
        shifts = jnp.where(row == 0, shift[0], jnp.where(row == 1, shift[1], shift[2]))
        for pair in range(tiles // 2):
            data = jnp.where(there, geo_halo[o, pair], 0.0)
            gammas = look_up(gamma, data)
            w8 = jnp.exp2(jnp.log(gammas) * (-1.5 / math.log(2.0))) * CUTOFF**-1.5
            chi8 = jnp.where(there, -look_up(electroneg, data), 0.0)
            if mine:
                eta8 = look_up(hardness, data)
            for half in range(2):
                u = pair * 2 + half
                entry = o * tiles + u
                r3 = half * 4 + 3
                raw = data if half == 0 else pltpu.roll(data, 4, 0)
                at = (raw + shifts) * scale
                norm = jnp.sum(jnp.where(row < 3, at * at, 0.0), axis=0, keepdims=True)
                norm = jnp.where(there, norm, FAR)
                at = jnp.where(there, at, 0.0)
                b = jnp.where(row < 3, -2.0 * at, jnp.where(row == 3, 1.0, jnp.where(row == 4, norm, 0.0)))
                b1, b2, b3 = split(b)
                features[entry] = jnp.concatenate([b1, b2, b1, b2, b3, b1], axis=0).astype(jnp.bfloat16)
                weights[pl.ds(entry, 1), :] = w8[r3 : r3 + 1]
                current0[pl.ds(entry, 1), :] = chi8[r3 : r3 + 1]
                current1[pl.ds(entry, 1), :] = jnp.where(there, jnp.full((1, width), -1.0, jnp.float32), 0.0)
                if mine:
                    a = jnp.where(row < 3, at, jnp.where(row == 3, norm, jnp.where(row == 4, 1.0, 0.0)))
                    a1, a2, a3 = split(a)
                    rows = jnp.concatenate(
                        [a1, a1, a2, a2, a1, a3, jnp.zeros((width - DEPTH, width), jnp.float32)], axis=0
                    )
                    lhs[u] = jnp.transpose(rows).astype(jnp.bfloat16)
                    weight_col[u] = jnp.transpose(jnp.broadcast_to(w8[r3 : r3 + 1], (width, width)))
                    eta_rows[pl.ds(u, 1), :] = eta8[r3 : r3 + 1]
                    gamma_rows[pl.ds(u, 1), :] = gammas[r3 : r3 + 1]

    pl.semaphore_wait(barrier, devices - 1)
    start_halo(geo_halo, geo_send, geo_recv)
    prepare(13, True)

    @pl.loop(0, 27)
    def _(o):
        where, there = neighbour(o)

        @pl.when(jnp.logical_and(there, o != 13))
        def _():
            halo_copy(geo_halo, geo_send, geo_recv, o, o, where).wait_recv()

        @pl.when(o != 13)
        def _():
            prepare(o, False)

    lanes_zero = jnp.zeros((width, width), jnp.float32)

    def row_sum(acc):
        return jnp.sum(jnp.transpose(acc), axis=0, keepdims=True)

    @pl.loop(0, tiles)
    def _(t):
        mine = lhs[t][:, :DEPTH]

        def step(g, carry):
            acc0, acc1, selves = carry
            for i in range(unroll):
                e = g * unroll + i
                entry = lists[t, e]
                x2 = jnp.dot(mine, features[entry], preferred_element_type=jnp.float32)
                x2 = jnp.maximum(x2, 1e-10)
                x = x2 * lax.rsqrt(x2)
                c = x2 * x + weight_col[t] * weights[pl.ds(entry, 1), :]
                inverse = jnp.exp2(jnp.log(c) * (-1.0 / (3.0 * math.log(2.0))))
                near = jnp.maximum(1.0 - x, 0.0)
                near = near * near
                f = COULOMB / CUTOFF
                taper = ((20.0 * f * x + 10.0 * f) * x + 4.0 * f) * x + f
                h = (near * near) * (taper * inverse)
                blocks[t * nbr + e] = h
                acc0 = acc0 + h * current0[pl.ds(entry, 1), :]
                acc1 = acc1 - h
                selves = selves + jnp.where(entry == 13 * tiles + t, 1, 0)
            return acc0, acc1, selves

        acc0, acc1, selves = lax.fori_loop(
            0, nbr // unroll, step, (lanes_zero, lanes_zero, jnp.int32(0))
        )
        image0[pl.ds(t, 1), :] = row_sum(acc0)
        image1[pl.ds(t, 1), :] = row_sum(acc1)
        diagonal[pl.ds(t, 1), :] = (
            eta_rows[pl.ds(t, 1), :]
            - selves.astype(jnp.float32) * COULOMB * gamma_rows[pl.ds(t, 1), :]
        )

    def couple():
        @pl.loop(0, tiles)
        def _(t):
            def step(g, carry):
                acc0, acc1 = carry
                for i in range(unroll):
                    e = g * unroll + i
                    entry = lists[t, e]
                    h = blocks[t * nbr + e]
                    acc0 = acc0 + h * current0[pl.ds(entry, 1), :]
                    acc1 = acc1 + h * current1[pl.ds(entry, 1), :]
                return acc0, acc1

            acc0, acc1 = lax.fori_loop(0, nbr // unroll, step, (lanes_zero, lanes_zero))
            image0[pl.ds(t, 1), :] = row_sum(acc0)
            image1[pl.ds(t, 1), :] = row_sum(acc1)

    systems = range(2)
    images = (image0, image1)
    currents = (current0, current1)
    diag = diagonal[...]
    r = [c[pl.ds(13 * tiles, tiles), :] for c in currents]
    w = [diag * r[s] + images[s][...] for s in systems]
    p = along = deep = None
    x = [jnp.zeros_like(r[0]) for s in systems]
    sum_x = [jnp.zeros((1, 1), jnp.float32) for s in systems]
    sum_p = rr_old = alpha = None
    for k in range(ITERS):
        parts = [
            jnp.where(
                lane == 0, total(r[s] * r[s]),
                jnp.where(lane == 1, total(r[s] * w[s]), jnp.where(lane == 2, total(r[s]), 0.0)),
            )
            for s in systems
        ]
        shares[k][0] = jnp.concatenate(parts, axis=0)
        last = k + 1 == ITERS
        if not last:
            buffer, send, recv = vec_halos[k], vec_sends[k], vec_recvs[k]
            for s in systems:
                buffer[13, s] = w[s]
            start_halo(buffer, send, recv)
        each_other(lambda j: sum_copy(k, devices - j, j).start())
        if not last:
            @pl.loop(0, 27)
            def _(o):
                where, there = neighbour(o)

                @pl.when(jnp.logical_and(there, o != 13))
                def _():
                    halo_copy(buffer, send, recv, o, o, where).wait_recv()

                start = pl.multiple_of(o * tiles, tiles)
                for s in systems:
                    currents[s][pl.ds(start, tiles), :] = jnp.where(there, buffer[o, s], 0.0)

            couple()
            q = [diag * w[s] + images[s][...] for s in systems]
        wait_shares(k, sum_recvs[k])
        sums = jnp.sum(shares[k][...], axis=0)
        rr, rw, sr = [
            [jnp.sum(jnp.where(lane == i, sums[s : s + 1], 0.0), axis=1, keepdims=True) for s in systems]
            for i in range(3)
        ]
        if k == 0:
            alpha = [rr[s] / rw[s] for s in systems]
            p, along, sum_p = list(r), list(w), sr
            if not last:
                deep = q
        else:
            beta = [rr[s] / rr_old[s] for s in systems]
            alpha = [rr[s] / (rw[s] - beta[s] * rr[s] / alpha[s]) for s in systems]
            p = [r[s] + beta[s] * p[s] for s in systems]
            sum_p = [sr[s] + beta[s] * sum_p[s] for s in systems]
            if not last:
                along = [w[s] + beta[s] * along[s] for s in systems]
                deep = [q[s] + beta[s] * deep[s] for s in systems]
        x = [x[s] + alpha[s] * p[s] for s in systems]
        sum_x = [sum_x[s] + alpha[s] * sum_p[s] for s in systems]
        rr_old = rr
        if not last:
            r = [r[s] - alpha[s] * along[s] for s in systems]
            w = [w[s] - alpha[s] * deep[s] for s in systems]

    charge = x[0] - (sum_x[0] / sum_x[1]) * x[1]
    for u in range(tiles):
        span = slice(u * width, (u + 1) * width)
        charges[0, 0, :, span] = charge[u : u + 1]
        for s in systems:
            solution_ref[0, 0, 0, s : s + 1, span] = x[s][u : u + 1]

    end_send(geo_halo, geo_send, geo_recv)
    for k in range(ITERS - 1):
        end_send(vec_halos[k], vec_sends[k], vec_recvs[k])
    for k in range(ITERS):
        wait_shares(k, sum_sends[k])


def on_device(positions, types, tile_lists, hardness, electroneg, gamma_table):
    atoms = positions.shape[4]
    tiles, nbr = tile_lists.shape
    width = atoms // tiles
    grid = tuple(lax.axis_size(a) for a in AXES)
    devices = math.prod(grid)
    unroll = next(u for u in (18, 16, 12, 8, 6, 4, 3, 2, 1) if nbr % u == 0)
    f32 = jnp.float32
    vmem = pl.BlockSpec(memory_space=pltpu.VMEM)
    smem = pl.BlockSpec(memory_space=pltpu.SMEM)
    rounds = ITERS - 1
    return pl.pallas_call(
        functools.partial(kernel, grid, unroll),
        out_shape=(
            jax.ShapeDtypeStruct((1, 1, 1, atoms), f32),
            jax.ShapeDtypeStruct((1, 1, 1, 2, atoms), f32),
        ),
        in_specs=[smem] * 4 + [vmem] * 2,
        out_specs=(vmem, vmem),
        scratch_shapes=[
            pltpu.VMEM((27, tiles // 2, 8, width), f32),
            [pltpu.VMEM((27, 2, tiles, width), f32)] * rounds,
            [pltpu.VMEM((devices, 2, width), f32)] * ITERS,
            pltpu.VMEM((27 * tiles, DEPTH, width), jnp.bfloat16),
            pltpu.VMEM((tiles, width, width), jnp.bfloat16),
            pltpu.VMEM((27 * tiles, width), f32),
            pltpu.VMEM((tiles, width, width), f32),
            pltpu.VMEM((27 * tiles, width), f32),
            pltpu.VMEM((27 * tiles, width), f32),
            pltpu.VMEM((tiles, width), f32),
            pltpu.VMEM((tiles, width), f32),
            pltpu.VMEM((tiles, width), f32),
            pltpu.VMEM((tiles, width), f32),
            pltpu.VMEM((tiles, width), f32),
            pltpu.VMEM((tiles * nbr, width, width), f32),
            pltpu.SemaphoreType.DMA((27,)),
            pltpu.SemaphoreType.DMA((27,)),
            [pltpu.SemaphoreType.DMA((27,))] * rounds,
            [pltpu.SemaphoreType.DMA((27,))] * rounds,
            [pltpu.SemaphoreType.DMA] * ITERS,
            [pltpu.SemaphoreType.DMA] * ITERS,
        ],
        compiler_params=pltpu.CompilerParams(
            collective_id=0, has_side_effects=True, vmem_limit_bytes=56 * 2**20
        ),
    )(tile_lists, hardness, electroneg, gamma_table, positions, types)


def solution(mesh):
    in_specs = (P("gx", "gy", "gz", None, None), P("gx", "gy", "gz", None), P(), P(), P(), P())
    out_specs = (P("gx", "gy", "gz", None), P("gx", "gy", "gz", None, None))
    return jax.shard_map(
        on_device, mesh=mesh, in_specs=in_specs, out_specs=out_specs, check_vma=False
    )
```

```python
import functools
import math

import jax
import jax.numpy as jnp
from jax import lax
from jax.experimental import pallas as pl
from jax.experimental.pallas import tpu as pltpu
from jax.sharding import PartitionSpec as P

ITERS = 4
CUTOFF = 10.0
COULOMB = 0.3
VOLUME = 10.0
MESH = pl.DeviceIdType.MESH
AXES = ("gx", "gy", "gz")
FAR = 100.0
DEPTH = 48


def total(a):
    return jnp.sum(jnp.sum(a, axis=0, keepdims=True), axis=1, keepdims=True)


def split(a):
    first = a.astype(jnp.bfloat16)
    rest = a - first.astype(jnp.float32)
    second = rest.astype(jnp.bfloat16)
    third = (rest - second.astype(jnp.float32)).astype(jnp.bfloat16)
    return [p.astype(jnp.float32) for p in (first, second, third)]


def kernel(
    grid, unroll, lists, hardness, electroneg, gamma, positions, types,
    charges, solution_ref,
    geo_halo, vec_halos, shares, features, lhs, weights, weight_col,
    current0, current1, eta_rows, gamma_rows, diagonal, image0, image1, blocks,
    geo_send, geo_recv, vec_sends, vec_recvs, sum_sends, sum_recvs,
):
    tiles, nbr = lists.shape
    kinds = gamma.shape[0]
    width = types.shape[3] // tiles
    devices = math.prod(grid)
    scale = (tiles * width * VOLUME) ** (1.0 / 3.0) / CUTOFF
    me = [lax.axis_index(a) for a in AXES]
    my_id = (me[0] * grid[1] + me[1]) * grid[2] + me[2]

    def device_of(d):
        return (d // (grid[1] * grid[2]), (d // grid[2]) % grid[1], d % grid[2])

    def neighbour(o):
        where = (me[0] + o // 9 - 1, me[1] + (o // 3) % 3 - 1, me[2] + o % 3 - 1)
        there = functools.reduce(
            jnp.logical_and,
            [jnp.logical_and(w >= 0, w < g) for w, g in zip(where, grid)],
        )
        return where, there

    barrier = pltpu.get_barrier_semaphore()

    @pl.loop(1, devices)
    def _(j):
        d = lax.rem(my_id + j, devices)
        pl.semaphore_signal(barrier, inc=1, device_id=device_of(d), device_id_type=MESH)


    def halo_copy(buffer, send, recv, slot, o, where):
        return pltpu.make_async_remote_copy(
            src_ref=buffer.at[13],
            dst_ref=buffer.at[slot],
            send_sem=send.at[o],
            recv_sem=recv.at[slot],
            device_id=where,
            device_id_type=MESH,
        )

    def each_neighbour(do):
        @pl.loop(0, 27, unroll=True)
        def _(o):
            where, there = neighbour(o)

            @pl.when(jnp.logical_and(there, o != 13))
            def _():
                do(o, where)

    def start_halo(buffer, send, recv):
        each_neighbour(lambda o, w: halo_copy(buffer, send, recv, 26 - o, o, w).start())

    def end_send(buffer, send, recv):
        each_neighbour(lambda o, w: halo_copy(buffer, send, recv, 26 - o, o, w).wait_send())

    def sum_copy(k, slot, j):
        return pltpu.make_async_remote_copy(
            src_ref=shares[k].at[0],
            dst_ref=shares[k].at[slot],
            send_sem=sum_sends[k],
            recv_sem=sum_recvs[k],
            device_id=device_of(lax.rem(my_id + j, devices)),
            device_id_type=MESH,
        )

    def wait_shares(k, sem):
        rest = shares[k].at[pl.ds(1, devices - 1)]
        pltpu.make_async_copy(rest, rest, sem).wait()

    def each_other(do):
        @pl.loop(1, devices)
        def _(j):
            do(j)

    for u in range(tiles):
        pair, top, span = u // 2, u % 2 * 4, slice(u * width, (u + 1) * width)
        geo_halo[13, pair, top : top + 3, :] = positions[0, 0, 0, :, span]
        geo_halo[13, pair, top + 3 : top + 4, :] = types[0, 0, :, span].astype(jnp.float32)

    row = lax.broadcasted_iota(jnp.int32, (8, width), 0)
    lane = lax.broadcasted_iota(jnp.int32, (1, width), 1)

    def look_up(table, kind):
        value = jnp.full(kind.shape, table[0], jnp.float32)
        for k in range(1, kinds):
            value = jnp.where(kind == float(k), table[k], value)
        return value

    def prepare(o, mine):
        where, there = neighbour(o)
        shift = [(o // 9 - 1), (o // 3) % 3 - 1, o % 3 - 1]
        shift = [s.astype(jnp.float32) - 0.5 if not mine else jnp.float32(-0.5) for s in shift]
        shifts = jnp.where(row == 0, shift[0], jnp.where(row == 1, shift[1], shift[2]))
        for pair in range(tiles // 2):
            data = jnp.where(there, geo_halo[o, pair], 0.0)
            gammas = look_up(gamma, data)
            w8 = jnp.exp2(jnp.log(gammas) * (-1.5 / math.log(2.0))) * CUTOFF**-1.5
            chi8 = jnp.where(there, -look_up(electroneg, data), 0.0)
            if mine:
                eta8 = look_up(hardness, data)
            for half in range(2):
                u = pair * 2 + half
                entry = o * tiles + u
                r3 = half * 4 + 3
                raw = data if half == 0 else pltpu.roll(data, 4, 0)
                at = (raw + shifts) * scale
                norm = jnp.sum(jnp.where(row < 3, at * at, 0.0), axis=0, keepdims=True)
                norm = jnp.where(there, norm, FAR)
                at = jnp.where(there, at, 0.0)
                b = jnp.where(row < 3, -2.0 * at, jnp.where(row == 3, 1.0, jnp.where(row == 4, norm, 0.0)))
                b1, b2, b3 = split(b)
                features[entry] = jnp.concatenate([b1, b2, b1, b2, b3, b1], axis=0).astype(jnp.bfloat16)
                weights[pl.ds(entry, 1), :] = w8[r3 : r3 + 1]
                current0[pl.ds(entry, 1), :] = chi8[r3 : r3 + 1]
                current1[pl.ds(entry, 1), :] = jnp.where(there, jnp.full((1, width), -1.0, jnp.float32), 0.0)
                if mine:
                    a = jnp.where(row < 3, at, jnp.where(row == 3, norm, jnp.where(row == 4, 1.0, 0.0)))
                    a1, a2, a3 = split(a)
                    rows = jnp.concatenate(
                        [a1, a1, a2, a2, a1, a3, jnp.zeros((width - DEPTH, width), jnp.float32)], axis=0
                    )
                    lhs[u] = jnp.transpose(rows).astype(jnp.bfloat16)
                    weight_col[u] = jnp.transpose(jnp.broadcast_to(w8[r3 : r3 + 1], (width, width)))
                    eta_rows[pl.ds(u, 1), :] = eta8[r3 : r3 + 1]
                    gamma_rows[pl.ds(u, 1), :] = gammas[r3 : r3 + 1]

    pl.semaphore_wait(barrier, devices - 1)
    start_halo(geo_halo, geo_send, geo_recv)
    prepare(13, True)

    @pl.loop(0, 27)
    def _(o):
        where, there = neighbour(o)

        @pl.when(jnp.logical_and(there, o != 13))
        def _():
            halo_copy(geo_halo, geo_send, geo_recv, o, o, where).wait_recv()

        @pl.when(o != 13)
        def _():
            prepare(o, False)

    lanes_zero = jnp.zeros((width, width), jnp.float32)

    def row_sum(acc):
        return jnp.sum(jnp.transpose(acc), axis=0, keepdims=True)

    @pl.loop(0, tiles)
    def _(t):
        mine = lhs[t][:, :DEPTH]

        def step(g, carry):
            acc0, acc1, selves = carry
            for i in range(unroll):
                e = g * unroll + i
                entry = lists[t, e]
                x2 = jnp.dot(mine, features[entry], preferred_element_type=jnp.float32)
                x2 = jnp.maximum(x2, 1e-10)
                x = x2 * lax.rsqrt(x2)
                c = x2 * x + weight_col[t] * weights[pl.ds(entry, 1), :]
                inverse = jnp.exp2(jnp.log(c) * (-1.0 / (3.0 * math.log(2.0))))
                near = jnp.maximum(1.0 - x, 0.0)
                near = near * near
                f = COULOMB / CUTOFF
                taper = ((20.0 * f * x + 10.0 * f) * x + 4.0 * f) * x + f
                h = (near * near) * (taper * inverse)
                blocks[t * nbr + e] = h
                acc0 = acc0 + h * current0[pl.ds(entry, 1), :]
                acc1 = acc1 - h
                selves = selves + jnp.where(entry == 13 * tiles + t, 1, 0)
            return acc0, acc1, selves

        acc0, acc1, selves = lax.fori_loop(
            0, nbr // unroll, step, (lanes_zero, lanes_zero, jnp.int32(0))
        )
        image0[pl.ds(t, 1), :] = row_sum(acc0)
        image1[pl.ds(t, 1), :] = row_sum(acc1)
        diagonal[pl.ds(t, 1), :] = (
            eta_rows[pl.ds(t, 1), :]
            - selves.astype(jnp.float32) * COULOMB * gamma_rows[pl.ds(t, 1), :]
        )

    def couple():
        @pl.loop(0, tiles)
        def _(t):
            def step(g, carry):
                acc0, acc1 = carry
                for i in range(unroll):
                    e = g * unroll + i
                    entry = lists[t, e]
                    h = blocks[t * nbr + e]
                    acc0 = acc0 + h * current0[pl.ds(entry, 1), :]
                    acc1 = acc1 + h * current1[pl.ds(entry, 1), :]
                return acc0, acc1

            acc0, acc1 = lax.fori_loop(0, nbr // unroll, step, (lanes_zero, lanes_zero))
            image0[pl.ds(t, 1), :] = row_sum(acc0)
            image1[pl.ds(t, 1), :] = row_sum(acc1)

    systems = range(2)
    images = (image0, image1)
    currents = (current0, current1)
    diag = diagonal[...]
    r = [c[pl.ds(13 * tiles, tiles), :] for c in currents]
    w = [diag * r[s] + images[s][...] for s in systems]
    p = along = deep = None
    x = [jnp.zeros_like(r[0]) for s in systems]
    sum_x = [jnp.zeros((1, 1), jnp.float32) for s in systems]
    sum_p = rr_old = alpha = None
    for k in range(ITERS):
        parts = [
            jnp.where(
                lane == 0, total(r[s] * r[s]),
                jnp.where(lane == 1, total(r[s] * w[s]), jnp.where(lane == 2, total(r[s]), 0.0)),
            )
            for s in systems
        ]
        shares[k][0] = jnp.concatenate(parts, axis=0)
        last = k + 1 == ITERS
        if not last:
            buffer, send, recv = vec_halos[k], vec_sends[k], vec_recvs[k]
            for s in systems:
                buffer[13, s] = w[s]
            start_halo(buffer, send, recv)
        each_other(lambda j: sum_copy(k, devices - j, j).start())
        if not last:
            @pl.loop(0, 27, unroll=True)
            def _(o):
                where, there = neighbour(o)

                @pl.when(jnp.logical_and(there, o != 13))
                def _():
                    halo_copy(buffer, send, recv, o, o, where).wait_recv()

                start = pl.multiple_of(o * tiles, tiles)
                for s in systems:
                    currents[s][pl.ds(start, tiles), :] = jnp.where(there, buffer[o, s], 0.0)

            couple()
            q = [diag * w[s] + images[s][...] for s in systems]
        wait_shares(k, sum_recvs[k])
        sums = jnp.sum(shares[k][...], axis=0)
        rr, rw, sr = [
            [jnp.sum(jnp.where(lane == i, sums[s : s + 1], 0.0), axis=1, keepdims=True) for s in systems]
            for i in range(3)
        ]
        if k == 0:
            alpha = [rr[s] / rw[s] for s in systems]
            p, along, sum_p = list(r), list(w), sr
            if not last:
                deep = q
        else:
            beta = [rr[s] / rr_old[s] for s in systems]
            alpha = [rr[s] / (rw[s] - beta[s] * rr[s] / alpha[s]) for s in systems]
            p = [r[s] + beta[s] * p[s] for s in systems]
            sum_p = [sr[s] + beta[s] * sum_p[s] for s in systems]
            if not last:
                along = [w[s] + beta[s] * along[s] for s in systems]
                deep = [q[s] + beta[s] * deep[s] for s in systems]
        x = [x[s] + alpha[s] * p[s] for s in systems]
        sum_x = [sum_x[s] + alpha[s] * sum_p[s] for s in systems]
        rr_old = rr
        if not last:
            r = [r[s] - alpha[s] * along[s] for s in systems]
            w = [w[s] - alpha[s] * deep[s] for s in systems]

    charge = x[0] - (sum_x[0] / sum_x[1]) * x[1]
    for u in range(tiles):
        span = slice(u * width, (u + 1) * width)
        charges[0, 0, :, span] = charge[u : u + 1]
        for s in systems:
            solution_ref[0, 0, 0, s : s + 1, span] = x[s][u : u + 1]

    end_send(geo_halo, geo_send, geo_recv)
    for k in range(ITERS - 1):
        end_send(vec_halos[k], vec_sends[k], vec_recvs[k])
    for k in range(ITERS):
        wait_shares(k, sum_sends[k])


def on_device(positions, types, tile_lists, hardness, electroneg, gamma_table):
    atoms = positions.shape[4]
    tiles, nbr = tile_lists.shape
    width = atoms // tiles
    grid = tuple(lax.axis_size(a) for a in AXES)
    devices = math.prod(grid)
    unroll = next(u for u in (18, 16, 12, 8, 6, 4, 3, 2, 1) if nbr % u == 0)
    f32 = jnp.float32
    vmem = pl.BlockSpec(memory_space=pltpu.VMEM)
    smem = pl.BlockSpec(memory_space=pltpu.SMEM)
    rounds = ITERS - 1
    return pl.pallas_call(
        functools.partial(kernel, grid, unroll),
        out_shape=(
            jax.ShapeDtypeStruct((1, 1, 1, atoms), f32),
            jax.ShapeDtypeStruct((1, 1, 1, 2, atoms), f32),
        ),
        in_specs=[smem] * 4 + [vmem] * 2,
        out_specs=(vmem, vmem),
        scratch_shapes=[
            pltpu.VMEM((27, tiles // 2, 8, width), f32),
            [pltpu.VMEM((27, 2, tiles, width), f32)] * rounds,
            [pltpu.VMEM((devices, 2, width), f32)] * ITERS,
            pltpu.VMEM((27 * tiles, DEPTH, width), jnp.bfloat16),
            pltpu.VMEM((tiles, width, width), jnp.bfloat16),
            pltpu.VMEM((27 * tiles, width), f32),
            pltpu.VMEM((tiles, width, width), f32),
            pltpu.VMEM((27 * tiles, width), f32),
            pltpu.VMEM((27 * tiles, width), f32),
            pltpu.VMEM((tiles, width), f32),
            pltpu.VMEM((tiles, width), f32),
            pltpu.VMEM((tiles, width), f32),
            pltpu.VMEM((tiles, width), f32),
            pltpu.VMEM((tiles, width), f32),
            pltpu.VMEM((tiles * nbr, width, width), f32),
            pltpu.SemaphoreType.DMA((27,)),
            pltpu.SemaphoreType.DMA((27,)),
            [pltpu.SemaphoreType.DMA((27,))] * rounds,
            [pltpu.SemaphoreType.DMA((27,))] * rounds,
            [pltpu.SemaphoreType.DMA] * ITERS,
            [pltpu.SemaphoreType.DMA] * ITERS,
        ],
        compiler_params=pltpu.CompilerParams(
            collective_id=0, has_side_effects=True, vmem_limit_bytes=56 * 2**20
        ),
    )(tile_lists, hardness, electroneg, gamma_table, positions, types)


def solution(mesh):
    in_specs = (P("gx", "gy", "gz", None, None), P("gx", "gy", "gz", None), P(), P(), P(), P())
    out_specs = (P("gx", "gy", "gz", None), P("gx", "gy", "gz", None, None))
    return jax.shard_map(
        on_device, mesh=mesh, in_specs=in_specs, out_specs=out_specs, check_vma=False
    )
```
